32 devices in a mesh: dp: 4 (over z), row: 4 (over y, x), col: 2 (over core).
Axes of the slice: x: 2, y: 2, z: 4, core: 2. Of those that a mesh axis runs over, the one named last changes fastest.
Arguments:
- hidden_in: bfloat16 [16384, 1024], P(('dp', 'row')), may hold values from -6 to 6
- segments: int32 [16384], P(('dp', 'row')), may hold values from 0 to 6, as said below
- mixer_gain: bfloat16 [1024], P(('dp', 'row')), may hold values from 0.25 to 1.75
- ssm_inner: bfloat16 [1024, 2, 1536], P(('dp', 'row'), None, 'col'), may hold values from -0.1875 to 0.1875
- state_proj: bfloat16 [1024, 256], P(('dp', 'row')), may hold values from -0.1875 to 0.1875
- step_proj: bfloat16 [1024, 24], P(('dp', 'row'), 'col'), may hold values from -0.1875 to 0.1875
- query_proj: bfloat16 [1024, 512], P(('dp', 'row'), 'col'), may hold values from -0.1875 to 0.1875
- key_value_projection: bfloat16 [1024, 2, 128], P(('dp', 'row'), None, 'col'), may hold values from -0.1875 to 0.1875
- conv_inner: float32 [4, 1536], P(None, 'col'), may hold values from -2.5 to 2.5
- conv_state: float32 [4, 256], replicated, may hold values from -2.5 to 2.5
- step_bias: float32 [24], P('col'), may hold values from -6 to -2
- decay_log: float32 [24], P('col'), may hold values from 0 to 3
- skip_gain: float32 [24], P('col'), may hold values from 0.5 to 1.5
- ssm_out: bfloat16 [1536, 1024], P('col', ('dp', 'row')), may hold values from -0.15625 to 0.15625
- attn_out: bfloat16 [512, 1024], P('col', ('dp', 'row')), may hold values from -1 to 1
- ffn_gain: bfloat16 [1024], P(('dp', 'row')), may hold values from 0.25 to 1.75
- gate_up: bfloat16 [1024, 2, 2048], P(('dp', 'row'), None, 'col'), may hold values from -0.1875 to 0.1875
- down_proj: bfloat16 [2048, 1024], P('col', ('dp', 'row')), may hold values from -0.125 to 0.125
- output_cotangent: bfloat16 [16384, 1024], P(('dp', 'row')), may hold values from -6 to 6
Outputs:
- hidden_out: bfloat16 [16384, 1024], P(('dp', 'row'))
- input_grad: float32 [16384, 1024], P(('dp', 'row'))
- grad_mixer_gain: float32 [1024], P(('dp', 'row'))
- grad_ssm_inner: float32 [1024, 2, 1536], P(('dp', 'row'), None, 'col')
- grad_state_proj: float32 [1024, 256], P(('dp', 'row'))
- grad_step_proj: float32 [1024, 24], P(('dp', 'row'), 'col')
- grad_query_proj: float32 [1024, 512], P(('dp', 'row'), 'col')
- grad_keyval_proj: float32 [1024, 2, 128], P(('dp', 'row'), None, 'col')
- grad_conv_inner: float32 [4, 1536], P(None, 'col')
- conv_state_gradient: float32 [4, 256], replicated
- grad_step_bias: float32 [24], P('col')
- grad_decay_log: float32 [24], P('col')
- grad_skip_gain: float32 [24], P('col')
- grad_ssm_out: float32 [1536, 1024], P('col', ('dp', 'row'))
- grad_attn_out: float32 [512, 1024], P('col', ('dp', 'row'))
- grad_ffn_gain: float32 [1024], P(('dp', 'row'))
- grad_gate_up: float32 [1024, 2, 2048], P(('dp', 'row'), None, 'col')
- grad_down_proj: float32 [2048, 1024], P('col', ('dp', 'row'))
The draws below stay inside these ranges and needn't reach their ends.
Inputs may be any that keep to these rules, and one draw needn't show every extreme that they name: `segments`: within each 1024-token sequence (tokens k * 1024 onward) the numbers start at 0, never fall and rise by one where a document starts; a document that starts and ends inside the sequence has 204 tokens or more.
All inputs are finite; a program needn't handle non-finite values.
Results may differ from the reference program's by a relative error of at most 0.018.
Values may be sent and summed in bfloat16 or wider, within the bound.
A program may use at most 320 MiB of HBM per device.

```python
import math
import jax
import jax.numpy as jnp
from jax import lax

MODEL_DIMENSION = 1024
HM = 24
HEAD_SIZE = 64
STATE = 128
HQ = 8
KEYVALUE_HEADS = 2
FF = 2048
CONV = 4
SEQ_LEN = 1024
SPAN = 256
QBLOCK = 512
DSSM = 1536
TOKENS = 16384


def draw_segments(key, part):
    key = jax.random.fold_in(key, 11)
    first_key, second_key, third_key = jax.random.split(key, 3)
    seq_count = TOKENS // SEQ_LEN
    first_start = jax.random.randint(first_key, (seq_count, 1), 1, 2 * SEQ_LEN + 1)
    lengths = jax.random.randint(second_key, (seq_count, 7), SEQ_LEN // 5, 2 * SEQ_LEN + 1)
    chosen = jax.random.randint(third_key, (), 0, seq_count)
    picked = (jnp.arange(seq_count, dtype=jnp.int32) == chosen)[:, None]
    first_start = jnp.where(picked, 1, first_start)
    lengths = jnp.where(picked, SEQ_LEN // 5, lengths)
    starts = jnp.concatenate([first_start, first_start + jnp.cumsum(lengths, axis=1)], 1)
    position = jnp.arange(SEQ_LEN, dtype=jnp.int32)
    numbers = jnp.sum((position[None, :, None] >= starts[:, None, :]).astype(jnp.int32), axis=-1)
    return numbers.reshape(TOKENS).astype(jnp.int32)


def block_levels(key, shape, cuts, low, top_value):
    level, own = 1.0, jax.random.fold_in(key, 6)
    for axis_at, shards_of in cuts:
        steps = jnp.exp(jax.random.uniform(jax.random.fold_in(own, axis_at), (shards_of,), jnp.float32, low / len(cuts), top_value / len(cuts)))
        level = level * jnp.repeat(steps, shape[axis_at] // shards_of).reshape([-1 if axis == axis_at else 1 for axis in range(len(shape))])
    return level


def normal_values(key, extent, deviation, bound, cuts=(), held_as=jnp.bfloat16):
    drawn = deviation * jax.random.normal(key, extent, jnp.float32)
    if cuts:
        drawn = drawn * block_levels(key, extent, cuts, -0.22, 0.18)
    return jnp.clip(drawn, -bound, bound).astype(held_as)


def setup_inputs(seed: int = 0) -> dict:
    arg_keys = jax.random.split(jax.random.key(seed), 20)
    return {
        "hidden_in": normal_values(arg_keys[0], (TOKENS, MODEL_DIMENSION), 1.0, 6.0, ((0, 16),)),
        "segments": draw_segments(jax.random.fold_in(arg_keys[19], 71), 0),
        "mixer_gain": jnp.clip(1.0 + 0.15 * jax.random.normal(arg_keys[2], (MODEL_DIMENSION,), jnp.float32), 0.25, 1.75).astype(jnp.bfloat16),
        "ssm_inner": normal_values(arg_keys[3], (MODEL_DIMENSION, 2, DSSM), MODEL_DIMENSION ** -0.5, 0.1875, ((0, 16), (2, 2))),
        "state_proj": normal_values(arg_keys[4], (MODEL_DIMENSION, 2 * STATE), MODEL_DIMENSION ** -0.5, 0.1875, ((0, 16),)),
        "step_proj": normal_values(arg_keys[5], (MODEL_DIMENSION, HM), MODEL_DIMENSION ** -0.5, 0.1875, ((0, 16), (1, 2))),
        "query_proj": normal_values(arg_keys[6], (MODEL_DIMENSION, HQ * HEAD_SIZE), MODEL_DIMENSION ** -0.5, 0.1875, ((0, 16), (1, 2))),
        "key_value_projection": normal_values(arg_keys[7], (MODEL_DIMENSION, 2, KEYVALUE_HEADS * HEAD_SIZE), MODEL_DIMENSION ** -0.5, 0.1875, ((0, 16), (2, 2))),
        "conv_inner": normal_values(arg_keys[8], (CONV, DSSM), 0.5, 2.5, ((1, 2),), jnp.float32),
        "conv_state": normal_values(arg_keys[9], (CONV, 2 * STATE), 0.5, 2.5, (), jnp.float32),
        "step_bias": jnp.clip(-6.0 + 4.0 * jax.random.uniform(arg_keys[10], (HM,), jnp.float32) ** block_levels(arg_keys[10], (HM,), ((0, 2),), -0.2, 0.2), -6.0, -2.0),
        "decay_log": jnp.clip(3.0 * jax.random.uniform(arg_keys[11], (HM,), jnp.float32) ** block_levels(arg_keys[11], (HM,), ((0, 2),), -0.2, 0.2), 0.0, 3.0),
        "skip_gain": jnp.clip(0.5 + 1.0 * jax.random.uniform(arg_keys[12], (HM,), jnp.float32) ** block_levels(arg_keys[12], (HM,), ((0, 2),), -0.2, 0.2), 0.5, 1.5),
        "ssm_out": normal_values(arg_keys[13], (DSSM, MODEL_DIMENSION), DSSM ** -0.5, 0.15625, ((0, 2), (1, 16))),
        "attn_out": normal_values(arg_keys[14], (HQ * HEAD_SIZE, MODEL_DIMENSION), (HQ * HEAD_SIZE // 16) ** -0.5, 1.0, ((0, 2), (1, 16))),
        "ffn_gain": jnp.clip(1.0 + 0.15 * jax.random.normal(arg_keys[15], (MODEL_DIMENSION,), jnp.float32), 0.25, 1.75).astype(jnp.bfloat16),
        "gate_up": normal_values(arg_keys[16], (MODEL_DIMENSION, 2, FF), MODEL_DIMENSION ** -0.5, 0.1875, ((0, 16), (2, 2))),
        "down_proj": normal_values(arg_keys[17], (FF, MODEL_DIMENSION), FF ** -0.5, 0.125, ((0, 2), (1, 16))),
        "output_cotangent": normal_values(arg_keys[18], (TOKENS, MODEL_DIMENSION), 1.0, 6.0, ((0, 16),)),
    }


EPS = 1e-05
THETA = 100000000000.0
HIGH = lax.Precision.HIGHEST

@jax.custom_vjp
def low(v):
    return lax.optimization_barrier(v.astype(jnp.bfloat16)).astype(jnp.float32)

@jax.custom_vjp
def low_back(v):
    return v

def low_keep(v):
    return (low(v), None)

def low_pass(kept, grad):
    return (grad,)

def back_keep(v):
    return (v, None)

def back_low(kept, grad):
    return (low(grad),)
low.defvjp(low_keep, low_pass)
low_back.defvjp(back_keep, back_low)

def causal_conv(signal, kernel, segment_ids):
    length = signal.shape[0]
    kernel_width = kernel.shape[0]
    summed = signal * kernel[kernel_width - 1][None, :]
    for offset in range(1, kernel_width):
        shifted = jnp.concatenate([jnp.zeros((offset, signal.shape[1]), signal.dtype), signal[:length - offset]], 0)
        earlier = jnp.concatenate([jnp.full((offset,), -1, segment_ids.dtype), segment_ids[:length - offset]], 0)
        matches = (earlier == segment_ids).astype(signal.dtype)
        summed = summed + shifted * kernel[kernel_width - 1 - offset][None, :] * matches[:, None]
    return summed

def state_scan(inner_heads, input_map, output_map, step_size, decay_rate, segment_ids):
    length, head_count, head_width = inner_heads.shape
    blocks = length // SPAN
    log_decay = step_size * decay_rate[None, :]
    inner_blocks = inner_heads.reshape(blocks, SPAN, head_count, head_width)
    input_blocks = input_map.reshape(blocks, SPAN, -1)
    output_blocks = output_map.reshape(blocks, SPAN, -1)
    step_blocks = step_size.reshape(blocks, SPAN, head_count)
    decay_blocks = log_decay.reshape(blocks, SPAN, head_count)
    segment_blocks = segment_ids.reshape(blocks, SPAN)
    previous = jnp.concatenate([segment_ids[:1], segment_blocks[:-1, -1]], 0)
    causal = jnp.arange(SPAN)[:, None] >= jnp.arange(SPAN)[None, :]

    def advance(carried, pieces):
        inner_part, input_part, output_part, step_part, decay_part, segment_part, before = pieces
        running = jnp.cumsum(decay_part, axis=0)
        spread = jnp.minimum(running[:, None, :] - running[None, :, :], 0.0)
        linked = (segment_part[:, None] == segment_part[None, :]) & causal
        kernel = jnp.where(linked[:, :, None], jnp.exp(spread), 0.0)
        intersection = jnp.dot(output_part, input_part.T, precision=HIGH)
        weights = kernel * intersection[:, :, None] * step_part[None, :, :]
        local_part = jnp.einsum('tsh,shp->thp', weights, inner_part, precision=HIGH)
        entering = (segment_part == before).astype(running.dtype)[:, None] * jnp.exp(running)
        from_state = jnp.einsum('tn,hpn->thp', output_part, carried, precision=HIGH) * entering[:, :, None]
        keeping = (segment_part[-1] == before).astype(running.dtype) * jnp.exp(running[-1])
        leaving = (segment_part == segment_part[-1]).astype(running.dtype)[:, None] * jnp.exp(running[-1][None, :] - running) * step_part
        updated = carried * keeping[:, None, None] + jnp.einsum('sh,shp,sn->hpn', leaving, inner_part, input_part, precision=HIGH)
        return (updated, local_part + from_state)
    initial = jnp.zeros((head_count, head_width, input_map.shape[1]), inner_heads.dtype)
    _, outputs = lax.scan(advance, initial, (inner_blocks, input_blocks, output_blocks, step_blocks, decay_blocks, segment_blocks, previous))
    return outputs.reshape(length, head_count, head_width)

def rotate(values):
    half_width = values.shape[-1] // 2
    position = jnp.arange(values.shape[0], dtype=jnp.float32)
    frequency = THETA ** (-2.0 * jnp.arange(half_width, dtype=jnp.float32) / values.shape[-1])
    angles = position[:, None] * frequency[None, :]
    cosine = jnp.cos(angles)[:, None, :]
    sine_part = jnp.sin(angles)[:, None, :]
    first_half = values[..., :half_width]
    second = values[..., half_width:]
    return jnp.concatenate([first_half * cosine - second * sine_part, second * cosine + first_half * sine_part], -1)

def attention(queries, keys_in, values_in, segment_ids):
    length, query_heads, head_width = queries.shape
    key_heads = keys_in.shape[1]
    grouped = queries.reshape(length, key_heads, query_heads // key_heads, head_width)
    position = jnp.arange(length, dtype=jnp.int32)
    score_scale = head_width ** (-0.5)

    def row_block(start):
        query_rows = lax.dynamic_slice_in_dim(grouped, start, QBLOCK, 0)
        segment_rows = lax.dynamic_slice_in_dim(segment_ids, start, QBLOCK, 0)
        row_positions = start + jnp.arange(QBLOCK, dtype=jnp.int32)
        scores = jnp.einsum('tkge,ske->kgts', query_rows, keys_in, precision=HIGH) * score_scale
        allowed = (segment_rows[:, None] == segment_ids[None, :]) & (row_positions[:, None] >= position[None, :])
        scores = jnp.where(allowed, scores, -1e+30)
        highest = lax.optimization_barrier(jnp.max(scores, axis=-1, keepdims=True))
        weights = jnp.exp(scores - highest)
        weights = weights / lax.optimization_barrier(jnp.sum(weights, axis=-1, keepdims=True))
        return jnp.einsum('kgts,ske->tkge', weights, values_in, precision=HIGH)
    starts = jnp.arange(length // QBLOCK, dtype=jnp.int32) * QBLOCK
    blocks = lax.map(jax.checkpoint(row_block), starts)
    return blocks.reshape(length, query_heads * head_width)

def mixer(inner_gate, state_in, step_raw, query, keyval, conv_inner, conv_state, step_bias, decay_log, skip_gain, segment_ids):
    length = inner_gate.shape[0]
    inner_width = inner_gate.shape[1] // 2
    head_count = step_raw.shape[1]
    gate_in = inner_gate[:, :inner_width]
    inner = jax.nn.silu(causal_conv(inner_gate[:, inner_width:], conv_inner, segment_ids))
    maps = jax.nn.silu(causal_conv(state_in, conv_state, segment_ids))
    state_width = maps.shape[1] // 2
    step_size = jax.nn.softplus(step_raw + step_bias[None, :])
    decay_rate = -jnp.exp(decay_log)
    inner_heads = inner.reshape(length, head_count, HEAD_SIZE)
    scanned = state_scan(inner_heads, maps[:, :state_width], maps[:, state_width:], step_size, decay_rate, segment_ids)
    scanned = scanned + skip_gain[None, :, None] * inner_heads
    ssm_part = scanned.reshape(length, inner_width) * jax.nn.silu(gate_in)
    kv_width = keyval.shape[1] // 2
    queries = rotate(query.reshape(length, -1, HEAD_SIZE))
    keys_in = rotate(keyval[:, :kv_width].reshape(length, -1, HEAD_SIZE))
    values_in = keyval[:, kv_width:].reshape(length, -1, HEAD_SIZE)
    attended = attention(queries, keys_in, values_in, segment_ids)
    return jnp.concatenate([ssm_part, attended], 1)

def rms_scale(values):
    return lax.rsqrt(lax.optimization_barrier(jnp.mean(values * values, axis=-1, keepdims=True)) + EPS)

def forward(weights, hidden, segment_ids):
    mixer_gain, ssm_inner, state_proj, step_proj, query_proj, key_value_projection, conv_inner, conv_state, step_bias, decay_log, skip_gain, ssm_out, attn_out, ffn_gain, gate_up, down_proj = weights
    row_count = hidden.shape[0]
    seq_count = row_count // SEQ_LEN
    normed = low(hidden * rms_scale(hidden) * mixer_gain)
    inner_gate = low_back(jnp.dot(normed, ssm_inner.reshape(MODEL_DIMENSION, -1), precision=HIGH))
    state_in = low_back(jnp.dot(normed, state_proj, precision=HIGH))
    step_raw = low_back(jnp.dot(normed, step_proj, precision=HIGH))
    query = low_back(jnp.dot(normed, query_proj, precision=HIGH))
    keyval = low_back(jnp.dot(normed, key_value_projection.reshape(MODEL_DIMENSION, -1), precision=HIGH))

    def single(leading_input, second_in, third_in, fourth_in, fifth_in, sequence_ids):
        return mixer(leading_input, second_in, third_in, fourth_in, fifth_in, conv_inner, conv_state, step_bias, decay_log, skip_gain, sequence_ids)
    mixed = jax.vmap(single)(inner_gate.reshape(seq_count, SEQ_LEN, -1), state_in.reshape(seq_count, SEQ_LEN, -1), step_raw.reshape(seq_count, SEQ_LEN, -1), query.reshape(seq_count, SEQ_LEN, -1), keyval.reshape(seq_count, SEQ_LEN, -1), segment_ids.reshape(seq_count, SEQ_LEN))
    mixed = low_back(low(mixed.reshape(row_count, -1)))
    mixer_delta = low_back(jnp.dot(mixed[:, :DSSM], ssm_out, precision=HIGH) + jnp.dot(mixed[:, DSSM:], attn_out, precision=HIGH))
    middle = hidden + mixer_delta
    normed_ffn = low(middle * rms_scale(middle) * ffn_gain)
    gate_values = low_back(jnp.dot(normed_ffn, gate_up.reshape(MODEL_DIMENSION, -1), precision=HIGH))
    hidden_ffn = low_back(low(jax.nn.silu(gate_values[:, :FF]) * gate_values[:, FF:]))
    return middle + jnp.dot(hidden_ffn, down_proj, precision=HIGH)

def reference(hidden_in, segments, mixer_gain, ssm_inner, state_proj, step_proj, query_proj, key_value_projection, conv_inner, conv_state, step_bias, decay_log, skip_gain, ssm_out, attn_out, ffn_gain, gate_up, down_proj, output_cotangent):
    weights = tuple((weight.astype(jnp.float32) for weight in (mixer_gain, ssm_inner, state_proj, step_proj, query_proj, key_value_projection, conv_inner, conv_state, step_bias, decay_log, skip_gain, ssm_out, attn_out, ffn_gain, gate_up, down_proj)))
    group_seqs = math.gcd(TOKENS // SEQ_LEN, 4)
    block_rows = group_seqs * SEQ_LEN
    block_count = TOKENS // block_rows
    hidden = hidden_in.astype(jnp.float32).reshape(block_count, block_rows, MODEL_DIMENSION)
    segment_blocks = segments.reshape(block_count, block_rows)
    cotangent = output_cotangent.astype(jnp.float32).reshape(block_count, block_rows, MODEL_DIMENSION)

    def scan_step(summed, pieces):
        hidden_part, segment_part, cotangent_part = pieces
        value, pullback = jax.vjp(lambda weight_set, rows_in: forward(weight_set, rows_in, segment_part), weights, hidden_part)
        weight_grads, hidden_grad = pullback(cotangent_part)
        summed = jax.tree.map(jnp.add, summed, weight_grads)
        return (summed, (value.astype(jnp.bfloat16), hidden_grad))
    zeros = jax.tree.map(jnp.zeros_like, weights)
    summed, (outputs, hidden_grads) = lax.scan(scan_step, zeros, (hidden, segment_blocks, cotangent))
    return (outputs.reshape(TOKENS, MODEL_DIMENSION), hidden_grads.reshape(TOKENS, MODEL_DIMENSION), summed[0], summed[1], summed[2], summed[3], summed[4], summed[5], summed[6], summed[7], summed[8], summed[9], summed[10], summed[11], summed[12], summed[13], summed[14], summed[15])
```

```python
import jax
import jax.numpy as jnp
from jax import lax
from jax.experimental import pallas as pl
from jax.experimental.pallas import tpu as pltpu
from jax.sharding import PartitionSpec as P

HEAD_SIZE = 64
SEQ_LEN = 1024
SPAN = 256


EPS = 1e-05
THETA = 100000000000.0
HIGH = lax.Precision.HIGHEST


def causal_conv(signal, kernel, segment_ids):
    length = signal.shape[0]
    kernel_width = kernel.shape[0]
    summed = signal * kernel[kernel_width - 1][None, :]
    for offset in range(1, kernel_width):
        shifted = jnp.concatenate(
            [jnp.zeros((offset, signal.shape[1]), signal.dtype), signal[: length - offset]], 0
        )
        earlier = jnp.concatenate(
            [jnp.full((offset,), -1, segment_ids.dtype), segment_ids[: length - offset]], 0
        )
        matches = (earlier == segment_ids).astype(signal.dtype)
        summed = summed + shifted * kernel[kernel_width - 1 - offset][None, :] * matches[:, None]
    return summed


def contract(left, right, left_dim, right_dim):
    return lax.dot_general(
        left.astype(jnp.bfloat16),
        right.astype(jnp.bfloat16),
        (((left_dim,), (right_dim,)), ((), ())),
        preferred_element_type=jnp.float32,
    )


def plain_nn(left, right):
    return contract(left, right, 1, 0)


def plain_nt(left, right):
    return contract(left, right, 1, 1)


def plain_tn(left, right):
    return contract(left, right, 0, 0)


def with_back(forward, back):
    wrapped = jax.custom_vjp(forward)
    wrapped.defvjp(lambda left, right: (forward(left, right), (left, right)), back)
    return wrapped


PLAIN = (plain_nn, plain_nt, plain_tn)
BACKED = (
    with_back(plain_nn, lambda kept, g: (plain_nt(g, kept[1]), plain_tn(kept[0], g))),
    with_back(plain_nt, lambda kept, g: (plain_nn(g, kept[1]), plain_tn(g, kept[0]))),
    with_back(plain_tn, lambda kept, g: (plain_nt(kept[1], g), plain_nn(kept[0], g))),
)
PAIR = 2
COLUMN_KINDS = 4
LANES = 128
VMEM_BYTES = 48 * 1024 * 1024


def causal_mask(segment_column, segment_row, row_start):
    shape = (segment_column.shape[0], segment_row.shape[1])
    rows = lax.broadcasted_iota(jnp.int32, shape, 0) + row_start
    columns = lax.broadcasted_iota(jnp.int32, shape, 1)
    return (segment_column == segment_row) & (rows >= columns)


def scan_math(pieces, masks, dots):
    product, product_right, product_left = dots
    inner, input_map, output_map, running, step, entering, leaving, running_row, keeping = pieces
    blocks = len(masks)
    outputs = [[None] * blocks for _ in range(PAIR)]
    carried = [None] * PAIR
    for block in range(blocks):
        intersection = product_right(output_map[block], input_map[block])
        for head in range(PAIR):
            part = inner[head][block]
            spread = running[head][block] - running_row[head][block]
            decay = jnp.exp(jnp.where(masks[block], spread, -1e30))
            result = product(decay * intersection, part * step[head][block])
            if block:
                result = result + (
                    product_right(output_map[block], carried[head]) * entering[head][block]
                )
            outputs[head][block] = result
            if block < blocks - 1:
                added = product_left(part * leaving[head][block], input_map[block])
                carried[head] = (
                    carried[head] * keeping[head][block] + added if block else added
                )
    return outputs


def scan_pieces(inner, input_map, output_map, columns, rows, segment_column, segment_row):
    blocks = inner.shape[0] // SPAN
    spans = [slice(SPAN * block, SPAN * (block + 1)) for block in range(blocks)]
    heads = range(PAIR)

    def column(kind):
        return [
            [columns[0, span, kind * PAIR + head : kind * PAIR + head + 1] for span in spans]
            for head in heads
        ]

    pieces = (
        [[inner[span, HEAD_SIZE * head : HEAD_SIZE * (head + 1)] for span in spans] for head in heads],
        [input_map[span, :] for span in spans],
        [output_map[span, :] for span in spans],
        column(0),
        column(1),
        column(2),
        column(3),
        [[rows[0, head : head + 1, span] for span in spans] for head in heads],
        [
            [rows[0, PAIR + head : PAIR + head + 1, span.start : span.start + LANES] for span in spans]
            for head in heads
        ],
    )
    masks = [causal_mask(segment_column[span, :], segment_row[:, span], 0) for span in spans]
    return pieces, masks, spans


def scan_forward_kernel(inner, input_map, output_map, columns, rows, seg_col, seg_row, out):
    pieces, masks, spans = scan_pieces(
        inner, input_map, output_map, columns, rows, seg_col, seg_row
    )
    results = scan_math(pieces, masks, PLAIN)
    for head in range(PAIR):
        for block, span in enumerate(spans):
            out[span, HEAD_SIZE * head : HEAD_SIZE * (head + 1)] = results[head][block]


def scan_backward_kernel(
    inner, input_map, output_map, columns, rows, seg_col, seg_row, cotangent,
    inner_grad, input_map_grad, output_map_grad, column_grad, row_grad,
):
    pieces, masks, spans = scan_pieces(
        inner, input_map, output_map, columns, rows, seg_col, seg_row
    )
    _, pullback = jax.vjp(lambda held: scan_math(held, masks, BACKED), pieces)
    (grads,) = pullback(
        [
            [cotangent[span, HEAD_SIZE * head : HEAD_SIZE * (head + 1)] for span in spans]
            for head in range(PAIR)
        ]
    )

    @pl.when(pl.program_id(0) == 0)
    def _():
        input_map_grad[...] = jnp.zeros_like(input_map_grad)
        output_map_grad[...] = jnp.zeros_like(output_map_grad)

    row_grad[...] = jnp.zeros_like(row_grad)
    for block, span in enumerate(spans):
        input_map_grad[span, :] += grads[1][block]
        output_map_grad[span, :] += grads[2][block]
        for head in range(PAIR):
            inner_grad[span, HEAD_SIZE * head : HEAD_SIZE * (head + 1)] = grads[0][head][block]
            for kind in range(COLUMN_KINDS):
                at = kind * PAIR + head
                column_grad[0, span, at : at + 1] = grads[3 + kind][head][block]
            row_grad[0, head : head + 1, span] = grads[7][head][block]
            row_grad[0, PAIR + head : PAIR + head + 1, span.start : span.start + LANES] = grads[8][
                head
            ][block]


def whole(array):
    return pl.BlockSpec(array.shape, lambda pair: (0,) * array.ndim)


def scan_specs(inner, input_map, output_map, columns, rows, seg_col, seg_row):
    return [
        pl.BlockSpec((inner.shape[0], PAIR * HEAD_SIZE), lambda pair: (0, pair)),
        whole(input_map),
        whole(output_map),
        pl.BlockSpec((1,) + columns.shape[1:], lambda pair: (pair, 0, 0)),
        pl.BlockSpec((1,) + rows.shape[1:], lambda pair: (pair, 0, 0)),
        whole(seg_col),
        whole(seg_row),
    ]


def run_kernel(body, operands, in_specs, outs, out_specs, grid, flops):
    return pl.pallas_call(
        body,
        grid=(grid,),
        in_specs=in_specs,
        out_specs=out_specs,
        out_shape=[jax.ShapeDtypeStruct(out.shape, jnp.float32) for out in outs],
        compiler_params=pltpu.CompilerParams(vmem_limit_bytes=VMEM_BYTES),
        cost_estimate=pl.CostEstimate(
            flops=flops, bytes_accessed=64 * 1024 * 1024, transcendentals=0
        ),
    )(*operands)


@jax.custom_vjp
def pair_scan(*operands):
    specs = scan_specs(*operands)
    return run_kernel(
        scan_forward_kernel,
        operands,
        specs,
        [operands[0]],
        [specs[0]],
        operands[3].shape[0],
        10**10,
    )[0]


def pair_scan_back(operands, cotangent):
    specs = scan_specs(*operands)
    grads = run_kernel(
        scan_backward_kernel,
        operands + (cotangent,),
        specs + [specs[0]],
        operands[:5],
        specs[:5],
        operands[3].shape[0],
        3 * 10**10,
    )
    return tuple(grads) + (jnp.zeros_like(operands[5]), jnp.zeros_like(operands[6]))


pair_scan.defvjp(lambda *operands: (pair_scan(*operands), operands), pair_scan_back)


def scan_columns(step_size, decay_rate, segments):
    length, heads = step_size.shape
    blocks = length // SPAN
    decay_blocks = (step_size * decay_rate[None, :]).reshape(blocks, SPAN, heads)
    lower = jnp.tril(jnp.ones((SPAN, SPAN), jnp.float32))
    running = jnp.einsum("ts,bsh->bth", lower, decay_blocks, precision=HIGH)
    last = running[:, -1:, :]
    segment_blocks = segments.reshape(blocks, SPAN)
    final = segment_blocks[:, -1]
    before = jnp.concatenate([segment_blocks[0, :1], final[:-1]], 0)
    enters = (segment_blocks == before[:, None]).astype(jnp.float32)[:, :, None]
    leaves = (segment_blocks == final[:, None]).astype(jnp.float32)[:, :, None]
    keeps = (final == before).astype(jnp.float32)[:, None, None]
    entering = (enters * jnp.exp(running)).reshape(length, heads)
    leaving = (leaves * jnp.exp(last - running)).reshape(length, heads) * step_size
    keeping = jnp.broadcast_to(keeps * jnp.exp(last), running.shape).reshape(length, heads)
    running = running.reshape(length, heads)
    pairs = heads // PAIR
    columns = jnp.stack([running, step_size, entering, leaving], 0)
    columns = columns.reshape(COLUMN_KINDS, length, pairs, PAIR).transpose(2, 1, 0, 3)
    rows = jnp.stack([running.T, keeping.T], 0).reshape(2, pairs, PAIR, length)
    rows = rows.transpose(1, 0, 2, 3).reshape(pairs, 2 * PAIR, length)
    return columns.reshape(pairs, length, COLUMN_KINDS * PAIR), rows


def attend_math(queries, keys_in, values_in, mask, dots):
    scores = jnp.where(mask, dots[1](queries, keys_in), -1e30)
    highest = lax.stop_gradient(jnp.max(scores, axis=-1, keepdims=True))
    weights = jnp.exp(scores - highest)
    total = jnp.sum(weights, axis=-1, keepdims=True)
    return dots[0](weights, values_in) / total


def attend_blocks(queries, seg_col, seg_row):
    for start in range(0, queries.shape[0], SPAN):
        rows = slice(start, start + SPAN)
        keys = slice(0, start + SPAN)
        mask = causal_mask(seg_col[rows, :], seg_row[:, keys], start)
        for head in range(PAIR):
            yield rows, keys, slice(HEAD_SIZE * head, HEAD_SIZE * (head + 1)), mask


def attend_forward_kernel(queries, keys_in, values_in, seg_col, seg_row, out):
    for rows, keys, lanes, mask in attend_blocks(queries, seg_col, seg_row):
        out[rows, lanes] = attend_math(
            queries[rows, lanes], keys_in[keys, :], values_in[keys, :], mask, PLAIN
        )


def attend_backward_kernel(
    queries, keys_in, values_in, seg_col, seg_row, cotangent, query_grad, key_grad, value_grad
):
    @pl.when(pl.program_id(0) == 0)
    def _():
        key_grad[...] = jnp.zeros_like(key_grad)
        value_grad[...] = jnp.zeros_like(value_grad)

    for rows, keys, lanes, mask in attend_blocks(queries, seg_col, seg_row):
        _, pullback = jax.vjp(
            lambda q, k, v: attend_math(q, k, v, mask, BACKED),
            queries[rows, lanes],
            keys_in[keys, :],
            values_in[keys, :],
        )
        query_part, key_part, value_part = pullback(cotangent[rows, lanes])
        query_grad[rows, lanes] = query_part
        key_grad[keys, :] += key_part
        value_grad[keys, :] += value_part


def attend_specs(queries, keys_in, values_in, seg_col, seg_row):
    return [
        pl.BlockSpec((queries.shape[0], PAIR * HEAD_SIZE), lambda pair: (0, pair)),
        whole(keys_in),
        whole(values_in),
        whole(seg_col),
        whole(seg_row),
    ]


@jax.custom_vjp
def attend(*operands):
    specs = attend_specs(*operands)
    pairs = operands[0].shape[1] // (PAIR * HEAD_SIZE)
    return run_kernel(
        attend_forward_kernel, operands, specs, [operands[0]], [specs[0]], pairs, 10**10
    )[0]


def attend_back(operands, cotangent):
    specs = attend_specs(*operands)
    pairs = operands[0].shape[1] // (PAIR * HEAD_SIZE)
    grads = run_kernel(
        attend_backward_kernel,
        operands + (cotangent,),
        specs + [specs[0]],
        operands[:3],
        specs[:3],
        pairs,
        3 * 10**10,
    )
    return tuple(grads) + (jnp.zeros_like(operands[3]), jnp.zeros_like(operands[4]))


attend.defvjp(lambda *operands: (attend(*operands), operands), attend_back)


def rotate(values):
    length, width = values.shape
    half = HEAD_SIZE // 2
    lane = jnp.arange(width, dtype=jnp.int32)
    position = jnp.arange(length, dtype=jnp.float32)
    frequency = THETA ** (-2.0 * jnp.arange(half, dtype=jnp.float32) / HEAD_SIZE)
    angles = position[:, None] * jnp.tile(frequency, width // half)[None, :]
    first = (lane % HEAD_SIZE < half)[None, :]
    later = jnp.concatenate([values[:, half:], values[:, :half]], 1)
    sooner = jnp.concatenate([values[:, -half:], values[:, :-half]], 1)
    return values * jnp.cos(angles) + jnp.where(first, -later, sooner) * jnp.sin(angles)


def mixer(
    inner_gate,
    state_in,
    step_raw,
    query,
    keyval,
    conv_inner,
    conv_state,
    step_bias,
    decay_log,
    skip_gain,
    segment_ids,
):
    inner_width = inner_gate.shape[1] // 2
    gate_in = inner_gate[:, :inner_width]
    inner = jax.nn.silu(causal_conv(inner_gate[:, inner_width:], conv_inner, segment_ids))
    maps = jax.nn.silu(causal_conv(state_in, conv_state, segment_ids))
    state_width = maps.shape[1] // 2
    step_size = jax.nn.softplus(step_raw + step_bias[None, :])
    decay_rate = -jnp.exp(decay_log)
    segment_float = segment_ids.astype(jnp.float32)
    seg_col, seg_row = segment_float[:, None], segment_float[None, :]
    columns, rows = scan_columns(step_size, decay_rate, segment_ids)
    scanned = pair_scan(
        inner, maps[:, :state_width], maps[:, state_width:], columns, rows, seg_col, seg_row
    )
    scanned = scanned + jnp.repeat(skip_gain, HEAD_SIZE)[None, :] * inner
    ssm_part = scanned * jax.nn.silu(gate_in)
    kv_width = keyval.shape[1] // 2
    attended = []
    key_heads = kv_width // HEAD_SIZE
    group = query.shape[1] // key_heads
    for head in range(key_heads):
        lanes = slice(HEAD_SIZE * head, HEAD_SIZE * (head + 1))
        attended.append(
            attend(
                rotate(query[:, group * head : group * (head + 1)] * HEAD_SIZE ** (-0.5)),
                rotate(keyval[:, :kv_width][:, lanes]),
                keyval[:, kv_width:][:, lanes],
                seg_col,
                seg_row,
            )
        )
    return jnp.concatenate([ssm_part] + attended, 1)


def rms_norm(values, gain):
    return values * lax.rsqrt(jnp.mean(values * values, axis=-1, keepdims=True) + EPS) * gain


def norm_back(values, gain, grad_normed):
    _, pullback = jax.vjp(rms_norm, values, gain)
    return pullback(grad_normed)


def matmul(left, right):
    return jnp.dot(left, right, preferred_element_type=jnp.float32)


def transposed_left(left, right):
    return lax.dot_general(
        left, right, (((0,), (0,)), ((), ())), preferred_element_type=jnp.float32
    )


def transposed_right(left, right):
    return lax.dot_general(
        left, right, (((1,), (1,)), ((), ())), preferred_element_type=jnp.float32
    )


SHARDS = ("dp", "row")


def pair_total(partial_value):
    own = partial_value.astype(jnp.bfloat16)
    other = lax.ppermute(own, "col", [(0, 1), (1, 0)])
    return own.astype(jnp.float32) + other.astype(jnp.float32)


def split_columns(array, widths):
    parts, start = [], 0
    for width in widths:
        parts.append(array[:, start : start + width])
        start += width
    return parts


def padded(parts):
    filled = sum(part.shape[1] for part in parts)
    gap = -filled % LANES
    return jnp.concatenate(
        list(parts) + [jnp.zeros((parts[0].shape[0], gap), parts[0].dtype)], 1
    )


def local(
    hidden_in,
    segments,
    mixer_gain,
    ssm_inner,
    state_proj,
    step_proj,
    query_proj,
    key_value_projection,
    conv_inner,
    conv_state,
    step_bias,
    decay_log,
    skip_gain,
    ssm_out,
    attn_out,
    ffn_gain,
    gate_up,
    down_proj,
    output_cotangent,
):
    share = ssm_inner.shape[0]
    in_parts = (
        ssm_inner.reshape(share, -1),
        state_proj,
        query_proj,
        key_value_projection.reshape(share, -1),
        step_proj,
        mixer_gain[:, None],
        ffn_gain[:, None],
    )
    in_widths = [part.shape[1] for part in in_parts]
    in_weight = lax.all_gather(padded(in_parts), SHARDS, axis=0, tiled=True)
    later_parts = (gate_up.reshape(share, -1), ssm_out.T, attn_out.T, down_proj.T)
    later_widths = [part.shape[1] for part in later_parts]
    later_weight = lax.all_gather(jnp.concatenate(later_parts, 1), SHARDS, axis=0, tiled=True)
    gain_mixer, gain_ffn = split_columns(in_weight, in_widths)[5:]
    gain_mixer, gain_ffn = gain_mixer[:, 0], gain_ffn[:, 0]
    gate_weight, ssm_weight, attn_weight, down_weight = split_columns(later_weight, later_widths)
    ssm_width = ssm_weight.shape[1]
    mixed_weight = later_weight[:, later_widths[0] : sum(later_widths[:3])]
    row_count = hidden_in.shape[0]
    model_width = hidden_in.shape[1]
    seq_count = row_count // SEQ_LEN
    segment_rows = segments.reshape(seq_count, SEQ_LEN)
    hidden = hidden_in.astype(jnp.float32)
    normed = rms_norm(hidden, gain_mixer.astype(jnp.float32)).astype(jnp.bfloat16)
    projected = matmul(normed, in_weight)
    inner_gate, state_in, query_in, keyval_in, step_raw = split_columns(projected, in_widths)[:5]

    def local_mixer(
        inner_part,
        state_part,
        step_part,
        query_part,
        keyval_part,
        inner_kernel,
        state_kernel,
        bias_part,
        decay_part,
        skip_part,
    ):

        def single(leading_input, second_in, third_in, fourth_in, fifth_in, sequence_ids):
            return mixer(
                leading_input,
                second_in,
                third_in,
                fourth_in,
                fifth_in,
                inner_kernel,
                state_kernel,
                bias_part,
                decay_part,
                skip_part,
                sequence_ids,
            )

        rows = []
        for index in range(seq_count):
            span = slice(index * SEQ_LEN, (index + 1) * SEQ_LEN)
            rows.append(
                single(
                    inner_part[span],
                    state_part[span],
                    step_part[span],
                    query_part[span],
                    keyval_part[span],
                    segment_rows[index],
                )
            )
        return jnp.concatenate(rows, 0)

    mixed_float, mixer_pull = jax.vjp(
        local_mixer,
        inner_gate,
        state_in,
        step_raw,
        query_in,
        keyval_in,
        conv_inner,
        conv_state,
        step_bias,
        decay_log,
        skip_gain,
    )
    mixed_out = mixed_float.astype(jnp.bfloat16)
    mixer_delta = pair_total(transposed_right(mixed_out, mixed_weight))
    middle = hidden + mixer_delta
    normed_ffn = rms_norm(middle, gain_ffn.astype(jnp.float32)).astype(jnp.bfloat16)
    gate_values = matmul(normed_ffn, gate_weight)
    half_width = gate_values.shape[1] // 2
    gate_part = gate_values[:, :half_width]
    up_part = gate_values[:, half_width:]
    hidden_ffn = (jax.nn.silu(gate_part) * up_part).astype(jnp.bfloat16)
    result = middle + pair_total(transposed_right(hidden_ffn, down_weight))
    hidden_out = result.astype(jnp.bfloat16)
    grad_down = transposed_left(output_cotangent, hidden_ffn)
    grad_hidden_ffn = (
        matmul(output_cotangent, down_weight).astype(jnp.bfloat16).astype(jnp.float32)
    )
    sigmoid_gate = jax.nn.sigmoid(gate_part)
    grad_gate = grad_hidden_ffn * up_part * sigmoid_gate * (1.0 + gate_part * (1.0 - sigmoid_gate))
    grad_up = grad_hidden_ffn * gate_part * sigmoid_gate
    grad_gate_values = jnp.concatenate([grad_gate, grad_up], 1).astype(jnp.bfloat16)
    grad_gate_weight = transposed_left(normed_ffn, grad_gate_values)
    grad_normed_ffn = pair_total(transposed_right(grad_gate_values, gate_weight))
    back_middle, grad_gain_ffn = norm_back(middle, gain_ffn.astype(jnp.float32), grad_normed_ffn)
    grad_middle = output_cotangent.astype(jnp.float32) + back_middle
    grad_delta = grad_middle.astype(jnp.bfloat16)
    grad_mixed_weight = transposed_left(grad_delta, mixed_out)
    later_grads = lax.psum_scatter(
        jnp.concatenate([grad_gate_weight, grad_mixed_weight, grad_down], 1).astype(jnp.bfloat16),
        SHARDS,
        scatter_dimension=0,
        tiled=True,
    ).astype(jnp.float32)
    grad_gate_up, grad_ssm_out, grad_attn_out, grad_down_proj = split_columns(
        later_grads, later_widths
    )
    grad_mixed = matmul(grad_delta, mixed_weight)
    grad_mixed = grad_mixed.astype(jnp.bfloat16).astype(jnp.float32)
    (
        grad_inner_gate,
        grad_state_in,
        raw_step_gradient,
        grad_query_in,
        grad_keyval_in,
        grad_conv_inner,
        conv_state_gradient,
        grad_step_bias,
        grad_decay_log,
        grad_skip_gain,
    ) = mixer_pull(grad_mixed)
    half_state = (0.5 * pair_total(grad_state_in)).astype(jnp.bfloat16)
    conv_state_gradient = conv_state_gradient + lax.ppermute(
        conv_state_gradient, "col", [(0, 1), (1, 0)]
    )
    small = (
        grad_conv_inner,
        conv_state_gradient,
        grad_step_bias,
        grad_decay_log,
        grad_skip_gain,
    )
    packed = lax.psum(jnp.concatenate([part.reshape(-1) for part in small]), SHARDS)
    unpacked, start = [], 0
    for part in small:
        unpacked.append(packed[start : start + part.size].reshape(part.shape))
        start += part.size
    grad_conv_inner, conv_state_gradient, grad_step_bias, grad_decay_log, grad_skip_gain = unpacked
    rounded = padded(
        [
            grad_inner_gate.astype(jnp.bfloat16),
            half_state,
            grad_query_in.astype(jnp.bfloat16),
            grad_keyval_in.astype(jnp.bfloat16),
            raw_step_gradient.astype(jnp.bfloat16),
            jnp.zeros((row_count, 2), jnp.bfloat16),
        ]
    )
    grad_normed = pair_total(transposed_right(rounded, in_weight))
    back_hidden, grad_gain_mixer = norm_back(hidden, gain_mixer.astype(jnp.float32), grad_normed)
    input_grad = grad_middle + back_hidden
    weight_grads = split_columns(transposed_left(normed, rounded), in_widths)[:5]
    weight_grads[1] = 2.0 * weight_grads[1]
    in_grads = lax.psum_scatter(
        padded(
            [
                part.astype(jnp.bfloat16)
                for part in weight_grads + [grad_gain_mixer[:, None], grad_gain_ffn[:, None]]
            ]
        ),
        SHARDS,
        scatter_dimension=0,
        tiled=True,
    ).astype(jnp.float32)
    (
        grad_ssm_inner,
        grad_state_proj,
        grad_query_proj,
        grad_keyval_proj,
        grad_step_proj,
        grad_mixer_gain,
        grad_ffn_gain,
    ) = split_columns(in_grads, in_widths)
    grad_ssm_inner = grad_ssm_inner.reshape(ssm_inner.shape)
    grad_keyval_proj = grad_keyval_proj.reshape(key_value_projection.shape)
    grad_gate_up = grad_gate_up.reshape(gate_up.shape)
    grad_mixer_gain, grad_ffn_gain = grad_mixer_gain[:, 0], grad_ffn_gain[:, 0]
    grad_ssm_out, grad_attn_out, grad_down_proj = (
        grad_ssm_out.T,
        grad_attn_out.T,
        grad_down_proj.T,
    )
    return (
        hidden_out,
        input_grad,
        grad_mixer_gain,
        grad_ssm_inner,
        grad_state_proj,
        grad_step_proj,
        grad_query_proj,
        grad_keyval_proj,
        grad_conv_inner,
        conv_state_gradient,
        grad_step_bias,
        grad_decay_log,
        grad_skip_gain,
        grad_ssm_out,
        grad_attn_out,
        grad_ffn_gain,
        grad_gate_up,
        grad_down_proj,
    )


def solution(mesh):
    placed = (
        P(("dp", "row"), None),
        P(("dp", "row")),
        P(("dp", "row")),
        P(("dp", "row"), None, "col"),
        P(("dp", "row"), None),
        P(("dp", "row"), "col"),
        P(("dp", "row"), "col"),
        P(("dp", "row"), None, "col"),
        P(None, "col"),
        P(),
        P("col"),
        P("col"),
        P("col"),
        P("col", ("dp", "row")),
        P("col", ("dp", "row")),
        P(("dp", "row")),
        P(("dp", "row"), None, "col"),
        P("col", ("dp", "row")),
        P(("dp", "row"), None),
    )
    return jax.shard_map(
        local,
        mesh=mesh,
        in_specs=placed,
        out_specs=(
            P(("dp", "row"), None),
            P(("dp", "row"), None),
            P(("dp", "row")),
            P(("dp", "row"), None, "col"),
            P(("dp", "row"), None),
            P(("dp", "row"), "col"),
            P(("dp", "row"), "col"),
            P(("dp", "row"), None, "col"),
            P(None, "col"),
            P(),
            P("col"),
            P("col"),
            P("col"),
            P("col", ("dp", "row")),
            P("col", ("dp", "row")),
            P(("dp", "row")),
            P(("dp", "row"), None, "col"),
            P("col", ("dp", "row")),
        ),
        check_vma=False,
    )
```

```python
import jax
import jax.numpy as jnp
from jax import lax
from jax.experimental import pallas as pl
from jax.experimental.pallas import tpu as pltpu
from jax.sharding import PartitionSpec as P

HEAD_SIZE = 64
SEQ_LEN = 1024
SPAN = 256


EPS = 1e-05
THETA = 100000000000.0
HIGH = lax.Precision.HIGHEST


def causal_conv(signal, kernel, segment_ids):
    length = signal.shape[0]
    kernel_width = kernel.shape[0]
    summed = signal * kernel[kernel_width - 1][None, :]
    for offset in range(1, kernel_width):
        shifted = jnp.concatenate(
            [jnp.zeros((offset, signal.shape[1]), signal.dtype), signal[: length - offset]], 0
        )
        earlier = jnp.concatenate(
            [jnp.full((offset,), -1, segment_ids.dtype), segment_ids[: length - offset]], 0
        )
        matches = (earlier == segment_ids).astype(signal.dtype)
        summed = summed + shifted * kernel[kernel_width - 1 - offset][None, :] * matches[:, None]
    return summed


def contract(left, right, left_dim, right_dim):
    return lax.dot_general(
        left.astype(jnp.bfloat16),
        right.astype(jnp.bfloat16),
        (((left_dim,), (right_dim,)), ((), ())),
        preferred_element_type=jnp.float32,
    )


def plain_nn(left, right):
    return contract(left, right, 1, 0)


def plain_nt(left, right):
    return contract(left, right, 1, 1)


def plain_tn(left, right):
    return contract(left, right, 0, 0)


def with_back(forward, back):
    wrapped = jax.custom_vjp(forward)
    wrapped.defvjp(lambda left, right: (forward(left, right), (left, right)), back)
    return wrapped


PLAIN = (plain_nn, plain_nt, plain_tn)
BACKED = (
    with_back(plain_nn, lambda kept, g: (plain_nt(g, kept[1]), plain_tn(kept[0], g))),
    with_back(plain_nt, lambda kept, g: (plain_nn(g, kept[1]), plain_tn(g, kept[0]))),
    with_back(plain_tn, lambda kept, g: (plain_nt(kept[1], g), plain_nn(kept[0], g))),
)
PAIR = 2
COLUMN_KINDS = 4
LANES = 128
VMEM_BYTES = 48 * 1024 * 1024


def causal_mask(segment_column, segment_row, row_start):
    shape = (segment_column.shape[0], segment_row.shape[1])
    rows = lax.broadcasted_iota(jnp.int32, shape, 0) + row_start
    columns = lax.broadcasted_iota(jnp.int32, shape, 1)
    return (segment_column == segment_row) & (rows >= columns)


def scan_math(pieces, masks, dots):
    product, product_right, product_left = dots
    inner, input_map, output_map, running, step, entering, leaving, running_row, keeping = pieces
    blocks = len(masks)
    outputs = [[None] * blocks for _ in range(PAIR)]
    carried = [None] * PAIR
    for block in range(blocks):
        intersection = product_right(output_map[block], input_map[block])
        for head in range(PAIR):
            part = inner[head][block]
            spread = running[head][block] - running_row[head][block]
            decay = jnp.exp(jnp.where(masks[block], spread, -1e30))
            result = product(decay * intersection, part * step[head][block])
            if block:
                result = result + (
                    product_right(output_map[block], carried[head]) * entering[head][block]
                )
            outputs[head][block] = result
            if block < blocks - 1:
                added = product_left(part * leaving[head][block], input_map[block])
                carried[head] = (
                    carried[head] * keeping[head][block] + added if block else added
                )
    return outputs


def scan_pieces(inner, input_map, output_map, columns, rows, segment_column, segment_row):
    blocks = inner.shape[0] // SPAN
    spans = [slice(SPAN * block, SPAN * (block + 1)) for block in range(blocks)]
    heads = range(PAIR)

    def column(kind):
        return [
            [columns[0, span, kind * PAIR + head : kind * PAIR + head + 1] for span in spans]
            for head in heads
        ]

    pieces = (
        [[inner[span, HEAD_SIZE * head : HEAD_SIZE * (head + 1)] for span in spans] for head in heads],
        [input_map[span, :] for span in spans],
        [output_map[span, :] for span in spans],
        column(0),
        column(1),
        column(2),
        column(3),
        [[rows[0, head : head + 1, span] for span in spans] for head in heads],
        [
            [rows[0, PAIR + head : PAIR + head + 1, span.start : span.start + LANES] for span in spans]
            for head in heads
        ],
    )
    masks = [causal_mask(segment_column[span, :], segment_row[:, span], 0) for span in spans]
    return pieces, masks, spans


def scan_forward_kernel(inner, input_map, output_map, columns, rows, seg_col, seg_row, out):
    pieces, masks, spans = scan_pieces(
        inner, input_map, output_map, columns, rows, seg_col, seg_row
    )
    results = scan_math(pieces, masks, PLAIN)
    for head in range(PAIR):
        for block, span in enumerate(spans):
            out[span, HEAD_SIZE * head : HEAD_SIZE * (head + 1)] = results[head][block]


def scan_backward_kernel(
    inner, input_map, output_map, columns, rows, seg_col, seg_row, cotangent,
    inner_grad, input_map_grad, output_map_grad, column_grad, row_grad,
):
    pieces, masks, spans = scan_pieces(
        inner, input_map, output_map, columns, rows, seg_col, seg_row
    )
    _, pullback = jax.vjp(lambda held: scan_math(held, masks, BACKED), pieces)
    (grads,) = pullback(
        [
            [cotangent[span, HEAD_SIZE * head : HEAD_SIZE * (head + 1)] for span in spans]
            for head in range(PAIR)
        ]
    )

    @pl.when(pl.program_id(0) == 0)
    def _():
        input_map_grad[...] = jnp.zeros_like(input_map_grad)
        output_map_grad[...] = jnp.zeros_like(output_map_grad)

    row_grad[...] = jnp.zeros_like(row_grad)
    for block, span in enumerate(spans):
        input_map_grad[span, :] += grads[1][block]
        output_map_grad[span, :] += grads[2][block]
        for head in range(PAIR):
            inner_grad[span, HEAD_SIZE * head : HEAD_SIZE * (head + 1)] = grads[0][head][block]
            for kind in range(COLUMN_KINDS):
                at = kind * PAIR + head
                column_grad[0, span, at : at + 1] = grads[3 + kind][head][block]
            row_grad[0, head : head + 1, span] = grads[7][head][block]
            row_grad[0, PAIR + head : PAIR + head + 1, span.start : span.start + LANES] = grads[8][
                head
            ][block]


def whole(array):
    return pl.BlockSpec(array.shape, lambda pair: (0,) * array.ndim)


def scan_specs(inner, input_map, output_map, columns, rows, seg_col, seg_row):
    return [
        pl.BlockSpec((inner.shape[0], PAIR * HEAD_SIZE), lambda pair: (0, pair)),
        whole(input_map),
        whole(output_map),
        pl.BlockSpec((1,) + columns.shape[1:], lambda pair: (pair, 0, 0)),
        pl.BlockSpec((1,) + rows.shape[1:], lambda pair: (pair, 0, 0)),
        whole(seg_col),
        whole(seg_row),
    ]


def run_kernel(body, operands, in_specs, outs, out_specs, grid, flops):
    return pl.pallas_call(
        body,
        grid=(grid,),
        in_specs=in_specs,
        out_specs=out_specs,
        out_shape=[jax.ShapeDtypeStruct(out.shape, jnp.float32) for out in outs],
        compiler_params=pltpu.CompilerParams(vmem_limit_bytes=VMEM_BYTES),
        cost_estimate=pl.CostEstimate(
            flops=flops, bytes_accessed=64 * 1024 * 1024, transcendentals=0
        ),
    )(*operands)


@jax.custom_vjp
def pair_scan(*operands):
    specs = scan_specs(*operands)
    return run_kernel(
        scan_forward_kernel,
        operands,
        specs,
        [operands[0]],
        [specs[0]],
        operands[3].shape[0],
        10**10,
    )[0]


def pair_scan_back(operands, cotangent):
    specs = scan_specs(*operands)
    grads = run_kernel(
        scan_backward_kernel,
        operands + (cotangent,),
        specs + [specs[0]],
        operands[:5],
        specs[:5],
        operands[3].shape[0],
        3 * 10**10,
    )
    return tuple(grads) + (jnp.zeros_like(operands[5]), jnp.zeros_like(operands[6]))


pair_scan.defvjp(lambda *operands: (pair_scan(*operands), operands), pair_scan_back)


def scan_columns(step_size, decay_rate, segments):
    length, heads = step_size.shape
    blocks = length // SPAN
    decay_blocks = (step_size * decay_rate[None, :]).reshape(blocks, SPAN, heads)
    lower = jnp.tril(jnp.ones((SPAN, SPAN), jnp.float32))
    running = jnp.einsum("ts,bsh->bth", lower, decay_blocks, precision=HIGH)
    last = running[:, -1:, :]
    segment_blocks = segments.reshape(blocks, SPAN)
    final = segment_blocks[:, -1]
    before = jnp.concatenate([segment_blocks[0, :1], final[:-1]], 0)
    enters = (segment_blocks == before[:, None]).astype(jnp.float32)[:, :, None]
    leaves = (segment_blocks == final[:, None]).astype(jnp.float32)[:, :, None]
    keeps = (final == before).astype(jnp.float32)[:, None, None]
    entering = (enters * jnp.exp(running)).reshape(length, heads)
    leaving = (leaves * jnp.exp(last - running)).reshape(length, heads) * step_size
    keeping = jnp.broadcast_to(keeps * jnp.exp(last), running.shape).reshape(length, heads)
    running = running.reshape(length, heads)
    pairs = heads // PAIR
    columns = jnp.stack([running, step_size, entering, leaving], 0)
    columns = columns.reshape(COLUMN_KINDS, length, pairs, PAIR).transpose(2, 1, 0, 3)
    rows = jnp.stack([running.T, keeping.T], 0).reshape(2, pairs, PAIR, length)
    rows = rows.transpose(1, 0, 2, 3).reshape(pairs, 2 * PAIR, length)
    return columns.reshape(pairs, length, COLUMN_KINDS * PAIR), rows


def attend_math(queries, keys_in, values_in, mask, dots):
    scores = jnp.where(mask, dots[1](queries, keys_in), -1e30)
    highest = lax.stop_gradient(jnp.max(scores, axis=-1, keepdims=True))
    weights = jnp.exp(scores - highest)
    total = jnp.sum(weights, axis=-1, keepdims=True)
    return dots[0](weights, values_in) / total


def attend_blocks(queries, seg_col, seg_row):
    for start in range(0, queries.shape[0], SPAN):
        rows = slice(start, start + SPAN)
        keys = slice(0, start + SPAN)
        mask = causal_mask(seg_col[rows, :], seg_row[:, keys], start)
        for head in range(PAIR):
            yield rows, keys, slice(HEAD_SIZE * head, HEAD_SIZE * (head + 1)), mask


def attend_forward_kernel(queries, keys_in, values_in, seg_col, seg_row, out):
    for rows, keys, lanes, mask in attend_blocks(queries, seg_col, seg_row):
        out[rows, lanes] = attend_math(
            queries[rows, lanes], keys_in[keys, :], values_in[keys, :], mask, PLAIN
        )


def attend_backward_kernel(
    queries, keys_in, values_in, seg_col, seg_row, cotangent, query_grad, key_grad, value_grad
):
    @pl.when(pl.program_id(0) == 0)
    def _():
        key_grad[...] = jnp.zeros_like(key_grad)
        value_grad[...] = jnp.zeros_like(value_grad)

    for rows, keys, lanes, mask in attend_blocks(queries, seg_col, seg_row):
        _, pullback = jax.vjp(
            lambda q, k, v: attend_math(q, k, v, mask, BACKED),
            queries[rows, lanes],
            keys_in[keys, :],
            values_in[keys, :],
        )
        query_part, key_part, value_part = pullback(cotangent[rows, lanes])
        query_grad[rows, lanes] = query_part
        key_grad[keys, :] += key_part
        value_grad[keys, :] += value_part


def attend_specs(queries, keys_in, values_in, seg_col, seg_row):
    return [
        pl.BlockSpec((queries.shape[0], PAIR * HEAD_SIZE), lambda pair: (0, pair)),
        whole(keys_in),
        whole(values_in),
        whole(seg_col),
        whole(seg_row),
    ]


@jax.custom_vjp
def attend(*operands):
    specs = attend_specs(*operands)
    pairs = operands[0].shape[1] // (PAIR * HEAD_SIZE)
    return run_kernel(
        attend_forward_kernel, operands, specs, [operands[0]], [specs[0]], pairs, 10**10
    )[0]


def attend_back(operands, cotangent):
    specs = attend_specs(*operands)
    pairs = operands[0].shape[1] // (PAIR * HEAD_SIZE)
    grads = run_kernel(
        attend_backward_kernel,
        operands + (cotangent,),
        specs + [specs[0]],
        operands[:3],
        specs[:3],
        pairs,
        3 * 10**10,
    )
    return tuple(grads) + (jnp.zeros_like(operands[3]), jnp.zeros_like(operands[4]))


attend.defvjp(lambda *operands: (attend(*operands), operands), attend_back)


def rotate(values):
    length, width = values.shape
    half = HEAD_SIZE // 2
    lane = jnp.arange(width, dtype=jnp.int32)
    position = jnp.arange(length, dtype=jnp.float32)
    frequency = THETA ** (-2.0 * jnp.arange(half, dtype=jnp.float32) / HEAD_SIZE)
    angles = position[:, None] * jnp.tile(frequency, width // half)[None, :]
    first = (lane % HEAD_SIZE < half)[None, :]
    later = jnp.concatenate([values[:, half:], values[:, :half]], 1)
    sooner = jnp.concatenate([values[:, -half:], values[:, :-half]], 1)
    return values * jnp.cos(angles) + jnp.where(first, -later, sooner) * jnp.sin(angles)


def mixer(
    inner_gate,
    state_in,
    step_raw,
    query,
    keyval,
    conv_inner,
    conv_state,
    step_bias,
    decay_log,
    skip_gain,
    segment_ids,
):
    inner_width = inner_gate.shape[1] // 2
    gate_in = inner_gate[:, :inner_width]
    inner = jax.nn.silu(causal_conv(inner_gate[:, inner_width:], conv_inner, segment_ids))
    maps = jax.nn.silu(causal_conv(state_in, conv_state, segment_ids))
    state_width = maps.shape[1] // 2
    step_size = jax.nn.softplus(step_raw + step_bias[None, :])
    decay_rate = -jnp.exp(decay_log)
    segment_float = segment_ids.astype(jnp.float32)
    seg_col, seg_row = segment_float[:, None], segment_float[None, :]
    columns, rows = scan_columns(step_size, decay_rate, segment_ids)
    scanned = pair_scan(
        inner, maps[:, :state_width], maps[:, state_width:], columns, rows, seg_col, seg_row
    )
    scanned = scanned + jnp.repeat(skip_gain, HEAD_SIZE)[None, :] * inner
    ssm_part = scanned * jax.nn.silu(gate_in)
    kv_width = keyval.shape[1] // 2
    attended = []
    key_heads = kv_width // HEAD_SIZE
    group = query.shape[1] // key_heads
    for head in range(key_heads):
        lanes = slice(HEAD_SIZE * head, HEAD_SIZE * (head + 1))
        attended.append(
            attend(
                rotate(query[:, group * head : group * (head + 1)] * HEAD_SIZE ** (-0.5)),
                rotate(keyval[:, :kv_width][:, lanes]),
                keyval[:, kv_width:][:, lanes],
                seg_col,
                seg_row,
            )
        )
    return jnp.concatenate([ssm_part] + attended, 1)


def rms_norm(values, gain):
    return values * lax.rsqrt(jnp.mean(values * values, axis=-1, keepdims=True) + EPS) * gain


def norm_back(values, gain, grad_normed):
    _, pullback = jax.vjp(rms_norm, values, gain)
    return pullback(grad_normed)


def matmul(left, right):
    return jnp.dot(left, right, preferred_element_type=jnp.float32)


def transposed_left(left, right):
    return lax.dot_general(
        left, right, (((0,), (0,)), ((), ())), preferred_element_type=jnp.float32
    )


def transposed_right(left, right):
    return lax.dot_general(
        left, right, (((1,), (1,)), ((), ())), preferred_element_type=jnp.float32
    )


SHARDS = ("dp", "row")


def pair_total(partial_value):
    own = partial_value.astype(jnp.bfloat16)
    other = lax.ppermute(own, "col", [(0, 1), (1, 0)])
    return own.astype(jnp.float32) + other.astype(jnp.float32)


def index_bits():
    bits = []
    for axis in ("row", "dp"):
        size = lax.psum(1, axis)
        bits += [(axis, 1 << power) for power in range(size.bit_length() - 1)]
    return bits


def partner_value(value, bit):
    axis, step = bit
    size = lax.psum(1, axis)
    return lax.ppermute(value, axis, [(index, index ^ step) for index in range(size)])


def all_sum(value):
    for bit in index_bits():
        value = value + partner_value(value, bit)
    return value


def scatter_sum(array):
    bits = index_bits()
    tiles = array.shape[1] // LANES
    edges = [LANES * (tiles * part // 3) for part in range(4)]
    results = []
    for part in range(3):
        left = bits[::-1]
        held = array[:, edges[part] : edges[part + 1]]
        held = held.reshape((2,) * len(bits) + (-1, held.shape[1]))
        for bit in bits[part:] + bits[:part]:
            at = left.index(bit)
            left.pop(at)
            mine = lax.axis_index(bit[0]) // bit[1] % 2
            sent = lax.dynamic_index_in_dim(held, 1 - mine, at, keepdims=False)
            kept = lax.dynamic_index_in_dim(held, mine, at, keepdims=False)
            got = partner_value(sent, bit)
            held = kept.astype(jnp.float32) + got.astype(jnp.float32)
            if left:
                held = held.astype(jnp.bfloat16)
        results.append(held)
    return jnp.concatenate(results, 1)


def split_columns(array, widths):
    parts, start = [], 0
    for width in widths:
        parts.append(array[:, start : start + width])
        start += width
    return parts


def padded(parts):
    filled = sum(part.shape[1] for part in parts)
    gap = -filled % LANES
    return jnp.concatenate(
        list(parts) + [jnp.zeros((parts[0].shape[0], gap), parts[0].dtype)], 1
    )


def local(
    hidden_in,
    segments,
    mixer_gain,
    ssm_inner,
    state_proj,
    step_proj,
    query_proj,
    key_value_projection,
    conv_inner,
    conv_state,
    step_bias,
    decay_log,
    skip_gain,
    ssm_out,
    attn_out,
    ffn_gain,
    gate_up,
    down_proj,
    output_cotangent,
):
    share = ssm_inner.shape[0]
    in_parts = (
        ssm_inner.reshape(share, -1),
        state_proj,
        query_proj,
        key_value_projection.reshape(share, -1),
        step_proj,
        mixer_gain[:, None],
        ffn_gain[:, None],
    )
    in_widths = [part.shape[1] for part in in_parts]
    in_weight = lax.all_gather(padded(in_parts), SHARDS, axis=0, tiled=True)
    later_parts = (gate_up.reshape(share, -1), ssm_out.T, attn_out.T, down_proj.T)
    later_widths = [part.shape[1] for part in later_parts]
    later_weight = lax.all_gather(jnp.concatenate(later_parts, 1), SHARDS, axis=0, tiled=True)
    gain_mixer, gain_ffn = split_columns(in_weight, in_widths)[5:]
    gain_mixer, gain_ffn = gain_mixer[:, 0], gain_ffn[:, 0]
    gate_weight, ssm_weight, attn_weight, down_weight = split_columns(later_weight, later_widths)
    ssm_width = ssm_weight.shape[1]
    mixed_weight = later_weight[:, later_widths[0] : sum(later_widths[:3])]
    row_count = hidden_in.shape[0]
    model_width = hidden_in.shape[1]
    seq_count = row_count // SEQ_LEN
    segment_rows = segments.reshape(seq_count, SEQ_LEN)
    hidden = hidden_in.astype(jnp.float32)
    normed = rms_norm(hidden, gain_mixer.astype(jnp.float32)).astype(jnp.bfloat16)
    projected = matmul(normed, in_weight)
    inner_gate, state_in, query_in, keyval_in, step_raw = split_columns(projected, in_widths)[:5]

    def local_mixer(
        inner_part,
        state_part,
        step_part,
        query_part,
        keyval_part,
        inner_kernel,
        state_kernel,
        bias_part,
        decay_part,
        skip_part,
    ):

        def single(leading_input, second_in, third_in, fourth_in, fifth_in, sequence_ids):
            return mixer(
                leading_input,
                second_in,
                third_in,
                fourth_in,
                fifth_in,
                inner_kernel,
                state_kernel,
                bias_part,
                decay_part,
                skip_part,
                sequence_ids,
            )

        rows = []
        for index in range(seq_count):
            span = slice(index * SEQ_LEN, (index + 1) * SEQ_LEN)
            rows.append(
                single(
                    inner_part[span],
                    state_part[span],
                    step_part[span],
                    query_part[span],
                    keyval_part[span],
                    segment_rows[index],
                )
            )
        return jnp.concatenate(rows, 0)

    mixed_float, mixer_pull = jax.vjp(
        local_mixer,
        inner_gate,
        state_in,
        step_raw,
        query_in,
        keyval_in,
        conv_inner,
        conv_state,
        step_bias,
        decay_log,
        skip_gain,
    )
    mixed_out = mixed_float.astype(jnp.bfloat16)
    mixer_delta = pair_total(transposed_right(mixed_out, mixed_weight))
    middle = hidden + mixer_delta
    normed_ffn = rms_norm(middle, gain_ffn.astype(jnp.float32)).astype(jnp.bfloat16)
    gate_values = matmul(normed_ffn, gate_weight)
    half_width = gate_values.shape[1] // 2
    gate_part = gate_values[:, :half_width]
    up_part = gate_values[:, half_width:]
    hidden_ffn = (jax.nn.silu(gate_part) * up_part).astype(jnp.bfloat16)
    result = middle + pair_total(transposed_right(hidden_ffn, down_weight))
    hidden_out = result.astype(jnp.bfloat16)
    grad_down = transposed_left(output_cotangent, hidden_ffn)
    grad_hidden_ffn = (
        matmul(output_cotangent, down_weight).astype(jnp.bfloat16).astype(jnp.float32)
    )
    sigmoid_gate = jax.nn.sigmoid(gate_part)
    grad_gate = grad_hidden_ffn * up_part * sigmoid_gate * (1.0 + gate_part * (1.0 - sigmoid_gate))
    grad_up = grad_hidden_ffn * gate_part * sigmoid_gate
    grad_gate_values = jnp.concatenate([grad_gate, grad_up], 1).astype(jnp.bfloat16)
    grad_gate_weight = transposed_left(normed_ffn, grad_gate_values)
    grad_normed_ffn = pair_total(transposed_right(grad_gate_values, gate_weight))
    back_middle, grad_gain_ffn = norm_back(middle, gain_ffn.astype(jnp.float32), grad_normed_ffn)
    grad_middle = output_cotangent.astype(jnp.float32) + back_middle
    grad_delta = grad_middle.astype(jnp.bfloat16)
    grad_mixed_weight = transposed_left(grad_delta, mixed_out)
    later_grads = scatter_sum(
        jnp.concatenate([grad_gate_weight, grad_mixed_weight, grad_down], 1).astype(jnp.bfloat16),
    )
    grad_gate_up, grad_ssm_out, grad_attn_out, grad_down_proj = split_columns(
        later_grads, later_widths
    )
    grad_mixed = matmul(grad_delta, mixed_weight)
    grad_mixed = grad_mixed.astype(jnp.bfloat16).astype(jnp.float32)
    (
        grad_inner_gate,
        grad_state_in,
        raw_step_gradient,
        grad_query_in,
        grad_keyval_in,
        grad_conv_inner,
        conv_state_gradient,
        grad_step_bias,
        grad_decay_log,
        grad_skip_gain,
    ) = mixer_pull(grad_mixed)
    half_state = (0.5 * pair_total(grad_state_in)).astype(jnp.bfloat16)
    conv_state_gradient = conv_state_gradient + lax.ppermute(
        conv_state_gradient, "col", [(0, 1), (1, 0)]
    )
    small = (
        grad_conv_inner,
        conv_state_gradient,
        grad_step_bias,
        grad_decay_log,
        grad_skip_gain,
    )
    packed = all_sum(jnp.concatenate([part.reshape(-1) for part in small]))
    unpacked, start = [], 0
    for part in small:
        unpacked.append(packed[start : start + part.size].reshape(part.shape))
        start += part.size
    grad_conv_inner, conv_state_gradient, grad_step_bias, grad_decay_log, grad_skip_gain = unpacked
    rounded = padded(
        [
            grad_inner_gate.astype(jnp.bfloat16),
            half_state,
            grad_query_in.astype(jnp.bfloat16),
            grad_keyval_in.astype(jnp.bfloat16),
            raw_step_gradient.astype(jnp.bfloat16),
            jnp.zeros((row_count, 2), jnp.bfloat16),
        ]
    )
    grad_normed = pair_total(transposed_right(rounded, in_weight))
    back_hidden, grad_gain_mixer = norm_back(hidden, gain_mixer.astype(jnp.float32), grad_normed)
    input_grad = grad_middle + back_hidden
    weight_grads = split_columns(transposed_left(normed, rounded), in_widths)[:5]
    weight_grads[1] = 2.0 * weight_grads[1]
    in_grads = scatter_sum(
        padded(
            [
                part.astype(jnp.bfloat16)
                for part in weight_grads + [grad_gain_mixer[:, None], grad_gain_ffn[:, None]]
            ]
        ),
    )
    (
        grad_ssm_inner,
        grad_state_proj,
        grad_query_proj,
        grad_keyval_proj,
        grad_step_proj,
        grad_mixer_gain,
        grad_ffn_gain,
    ) = split_columns(in_grads, in_widths)
    grad_ssm_inner = grad_ssm_inner.reshape(ssm_inner.shape)
    grad_keyval_proj = grad_keyval_proj.reshape(key_value_projection.shape)
    grad_gate_up = grad_gate_up.reshape(gate_up.shape)
    grad_mixer_gain, grad_ffn_gain = grad_mixer_gain[:, 0], grad_ffn_gain[:, 0]
    grad_ssm_out, grad_attn_out, grad_down_proj = (
        grad_ssm_out.T,
        grad_attn_out.T,
        grad_down_proj.T,
    )
    return (
        hidden_out,
        input_grad,
        grad_mixer_gain,
        grad_ssm_inner,
        grad_state_proj,
        grad_step_proj,
        grad_query_proj,
        grad_keyval_proj,
        grad_conv_inner,
        conv_state_gradient,
        grad_step_bias,
        grad_decay_log,
        grad_skip_gain,
        grad_ssm_out,
        grad_attn_out,
        grad_ffn_gain,
        grad_gate_up,
        grad_down_proj,
    )


def solution(mesh):
    placed = (
        P(("dp", "row"), None),
        P(("dp", "row")),
        P(("dp", "row")),
        P(("dp", "row"), None, "col"),
        P(("dp", "row"), None),
        P(("dp", "row"), "col"),
        P(("dp", "row"), "col"),
        P(("dp", "row"), None, "col"),
        P(None, "col"),
        P(),
        P("col"),
        P("col"),
        P("col"),
        P("col", ("dp", "row")),
        P("col", ("dp", "row")),
        P(("dp", "row")),
        P(("dp", "row"), None, "col"),
        P("col", ("dp", "row")),
        P(("dp", "row"), None),
    )
    return jax.shard_map(
        local,
        mesh=mesh,
        in_specs=placed,
        out_specs=(
            P(("dp", "row"), None),
            P(("dp", "row"), None),
            P(("dp", "row")),
            P(("dp", "row"), None, "col"),
            P(("dp", "row"), None),
            P(("dp", "row"), "col"),
            P(("dp", "row"), "col"),
            P(("dp", "row"), None, "col"),
            P(None, "col"),
            P(),
            P("col"),
            P("col"),
            P("col"),
            P("col", ("dp", "row")),
            P("col", ("dp", "row")),
            P(("dp", "row")),
            P(("dp", "row"), None, "col"),
            P("col", ("dp", "row")),
        ),
        check_vma=False,
    )
```
